32 devices in a mesh: groups: 2 (over y), gx: 4 (over z), gy: 4 (over x, core).
Axes of the slice: x: 2, y: 2, z: 4, core: 2. Of those that a mesh axis runs over, the one named last changes fastest.
Arguments:
- rows_in: bfloat16 [384, 8192], P(('groups', 'gy'), 'gx'), parts along dimension 0, may hold values from -6 to 6
- gate_weight: bfloat16 [8192, 20480], P('gx', 'gy'), may hold values from -0.09375 to 0.09375
- up_weight: bfloat16 [8192, 20480], P('gx', 'gy'), may hold values from -0.09375 to 0.09375
- down_weight: bfloat16 [20480, 8192], P('gy', 'gx'), may hold values from -0.0625 to 0.0625
- gate_keep: int32 [64, 160], P('gx', 'gy'), may hold values 0 or 1
- up_keep: int32 [64, 160], P('gx', 'gy'), may hold values 0 or 1
- down_keep: int32 [160, 64], P('gy', 'gx'), may hold values 0 or 1
Outputs:
- mixed: bfloat16 [384, 8192], P(('groups', 'gy'), 'gx'), parts along dimension 0
The draws below stay inside these ranges and needn't reach their ends.
There are 2 independent parts, one for each index of `groups`. The reference program is written for one: setup_inputs(seed, part) draws one part's arguments, and reference() takes and returns one part's arrays. A program takes and returns all parts, laid end to end along the dimension named above; an argument that names none is the same for every part. Nothing has to cross between parts.
All inputs are finite; a program needn't handle non-finite values. No bound on the sum of `gate_keep` or of `up_keep` or of `down_keep` on one device may be relied on, other than what follows from the above.
Results may differ from the reference program's by a relative error of at most 0.02.
Values may be sent and summed in bfloat16 or wider, within the bound.
A program may use at most 256 MiB of HBM per device.

```python
import jax
import jax.numpy as jnp
from jax import lax

D = 8192
FF = 20480
BLOCK = 128
ROWS = 192
N_GX = 4
N_GY = 4


def touch_ends(values, own_key, least, top_value):
    extent = values.shape
    index_at = [jax.random.randint(jax.random.fold_in(own_key, axis), (), 0, extent[axis]) for axis in range(len(extent))]
    values = values.at[tuple(index_at)].set(least)
    longest = extent.index(max(extent))
    index_at[longest] = (index_at[longest] + 1) % extent[longest]
    return values.at[tuple(index_at)].set(top_value)


def raised(drawn, rng, source, target, blocks, factor):
    owner, partner = [(jnp.arange(drawn.shape[dim]) // (drawn.shape[dim] // blocks)).reshape([-1 if axis == dim else 1 for axis in range(drawn.ndim)]) for dim in (source, target)]
    chosen = jax.random.permutation(rng, blocks)[partner]
    strong = (owner == chosen) | (owner == (partner + blocks // 2) % blocks)
    return jnp.where(strong, factor * drawn, drawn)


def block_scale(key, dims, cuts, least, largest):
    loudness, own = 1.0, jax.random.fold_in(key, 6)
    for position, blocks in cuts:
        heights = jnp.exp(jax.random.uniform(jax.random.fold_in(own, position), (blocks,), jnp.float32, least / len(cuts), largest / len(cuts)))
        loudness = loudness * jnp.repeat(heights, dims[position] // blocks).reshape([-1 if axis == position else 1 for axis in range(len(dims))])
    return loudness


def scatter_about(rng, shape, scale, limit, shards=(), kind=jnp.bfloat16):
    entries = jax.random.normal(rng, shape, jnp.float32) * scale
    if len(shards) > 0:
        entries = block_scale(rng, shape, shards, -0.22, 0.18) * entries
    return jnp.clip(entries, min=-limit, max=limit).astype(kind)


def heavy_noise(stream_key, shape, spread, limit, cuts, heavy, held_as=jnp.bfloat16):
    result = spread * jax.random.normal(stream_key, shape, jnp.float32)
    if cuts:
        result = result * block_scale(stream_key, shape, cuts, -0.22, 0.18)
    return jnp.clip(raised(result, jax.random.fold_in(stream_key, 3), *heavy), -limit, limit).astype(held_as)


def setup_inputs(seed: int = 0, part: int = 0) -> dict:
    streams_of = jax.random.split(jax.random.key(seed), 8)
    part_splits = jax.random.split(jax.random.fold_in(streams_of[7], part), 8)
    return {
        "rows_in": heavy_noise(part_splits[0], (ROWS, D), 1.0, 6.0, ((0, 4), (1, 4)), (1, 0, 4, 2.0)),
        "gate_weight": scatter_about(streams_of[1], (D, FF), (D // 2) ** -0.5, 0.09375, ((0, 4), (1, 4))),
        "up_weight": scatter_about(streams_of[2], (D, FF), (D // 2) ** -0.5, 0.09375, ((0, 4), (1, 4))),
        "down_weight": scatter_about(streams_of[3], (FF, D), (FF // 2) ** -0.5, 0.0625, ((0, 4), (1, 4))),
        "gate_keep": touch_ends((jax.random.randint(streams_of[4], (D // BLOCK, FF // BLOCK), 0, 2) < 1).astype(jnp.int32), jax.random.fold_in(streams_of[4], 1), 0, 1),
        "up_keep": touch_ends((jax.random.randint(streams_of[5], (D // BLOCK, FF // BLOCK), 0, 2) < 1).astype(jnp.int32), jax.random.fold_in(streams_of[5], 1), 0, 1),
        "down_keep": touch_ends((jax.random.randint(streams_of[6], (FF // BLOCK, D // BLOCK), 0, 2) < 1).astype(jnp.int32), jax.random.fold_in(streams_of[6], 1), 0, 1),
    }


def expand_mask(keep_mask, weights):
    grown = jnp.repeat(jnp.repeat(keep_mask, BLOCK, axis=0), BLOCK, axis=1)
    return weights * grown.astype(weights.dtype)


def rounded_pieces(activations, weights, pieces):
    row_count = activations.shape[0]
    inner = activations.shape[1] // pieces
    left_parts = activations.reshape(row_count, pieces, inner).transpose(1, 0, 2)
    right_parts = weights.reshape(pieces, inner, weights.shape[1])

    def accumulate(running, couple):
        product = jnp.dot(couple[0], couple[1], preferred_element_type=jnp.float32)
        rounded = lax.optimization_barrier(product.astype(jnp.bfloat16))
        return running + rounded.astype(jnp.float32), None

    start_total = jnp.zeros((row_count, weights.shape[1]), jnp.float32)
    running, unused = lax.scan(accumulate, start_total, (left_parts, right_parts))
    return running


def reference(rows_in, gate_weight, up_weight, down_weight, gate_keep, up_keep, down_keep):
    pruned_gate = expand_mask(gate_keep, gate_weight)
    pruned_up = expand_mask(up_keep, up_weight)
    pruned_down = expand_mask(down_keep, down_weight)
    gate = rounded_pieces(rows_in, pruned_gate, N_GX)
    up = rounded_pieces(rows_in, pruned_up, N_GX)
    hidden = (jax.nn.silu(gate) * up).astype(jnp.bfloat16)
    mixed = rounded_pieces(hidden, pruned_down, N_GY)
    return mixed.astype(jnp.bfloat16)
```

```python
import functools

import jax
import jax.numpy as jnp
from jax import lax
from jax.experimental import pallas as pl
from jax.experimental.pallas import tpu as pltpu
from jax.sharding import PartitionSpec as P

BLOCK = 128
CHUNK = 256
SLOTS = 3
SKEW_SUM = 1
SKEW_HID = 1
MESH = pl.DeviceIdType.MESH


def ffn_kernel(
    n, peers, steps_per_way,
    x_ref, gate_ref, up_ref, down_ref, gate_keep, up_keep, down_keep,
    out_ref,
    gathered, rows, weights, down, sums, own, hid, total, leaving, landing,
    row_send, row_recv, row_local, weight_sem, down_sem,
    sum_send, sum_recv, hid_send, hid_recv, out_send, out_recv,
):
    z = lax.axis_index("gx")
    y = lax.axis_index("gy")
    own_rows, depth = x_ref.shape
    all_rows = peers * own_rows
    width = down_ref.shape[1]
    per_way = steps_per_way

    def pos_of(way):
        return jnp.where(way == 0, z, n - 1 - z)

    def onward(way):
        return jnp.where(way == 0, z + 1, z - 1)

    def backward(way):
        return jnp.where(way == 0, z - 1, z + 1)

    def weight_copies(way, j):
        slot = lax.rem(j, SLOTS)
        start = pl.multiple_of((way * per_way + j) * CHUNK, CHUNK)
        return [
            pltpu.make_async_copy(
                source.at[:, pl.ds(start, CHUNK)],
                weights.at[way, slot, :, pl.ds(side * CHUNK, CHUNK)],
                weight_sem.at[way, slot, side],
            )
            for side, source in enumerate((gate_ref, up_ref))
        ]

    def down_copy(way, j):
        start = pl.multiple_of((way * per_way + j) * CHUNK, CHUNK)
        return pltpu.make_async_copy(
            down_ref.at[pl.ds(start, CHUNK), :], down.at[way, j], down_sem.at[way, j]
        )

    def sum_copy(way, j):
        return pltpu.make_async_remote_copy(
            sums.at[way, j], sums.at[way, j], sum_send.at[way, j], sum_recv.at[way, j],
            device_id={"gx": onward(way)}, device_id_type=MESH,
        )

    def hid_copy(way, j):
        return pltpu.make_async_remote_copy(
            hid.at[way, j], hid.at[way, j], hid_send.at[way, j], hid_recv.at[way, j],
            device_id={"gx": backward(way)}, device_id_type=MESH,
        )

    def row_copy(sender, receiver):
        return pltpu.make_async_remote_copy(
            x_ref, gathered.at[sender], row_send.at[receiver], row_recv.at[sender],
            device_id={"gy": receiver}, device_id_type=MESH,
        )

    def out_copy(sender, receiver):
        return pltpu.make_async_remote_copy(
            leaving.at[receiver], landing.at[sender], out_send.at[receiver], out_recv.at[sender],
            device_id={"gy": receiver}, device_id_type=MESH,
        )

    barrier = pltpu.get_barrier_semaphore()
    for step in range(1, peers):
        pl.semaphore_signal(
            barrier, inc=1, device_id={"gy": lax.rem(y + step, peers)}, device_id_type=MESH
        )

    @pl.when(z > 0)
    def _():
        pl.semaphore_signal(barrier, inc=1, device_id={"gx": z - 1}, device_id_type=MESH)

    @pl.when(z < n - 1)
    def _():
        pl.semaphore_signal(barrier, inc=1, device_id={"gx": z + 1}, device_id_type=MESH)

    local = pltpu.make_async_copy(x_ref, gathered.at[y], row_local)
    local.start()
    for way in range(2):
        for j in range(min(SLOTS, per_way)):
            for copy in weight_copies(way, j):
                copy.start()
    pl.semaphore_wait(barrier, peers - 1 + jnp.where(z > 0, 1, 0) + jnp.where(z < n - 1, 1, 0))

    for step in range(1, peers):
        row_copy(y, lax.rem(y + step, peers)).start()
    local.wait()
    total[...] = jnp.zeros_like(total)
    for step in range(1, peers):
        row_copy(lax.rem(y + step, peers), y).wait_recv()
    if own_rows % 16 == 0:
        for part in range(peers):
            rows[part * own_rows:(part + 1) * own_rows, :] = gathered[part]
    else:
        rows[...] = jnp.concatenate(
            [gathered[part].astype(jnp.float32) for part in range(peers)], axis=0
        ).astype(rows.dtype)

    def mask_tile(keep):
        return jnp.full((16, BLOCK), keep.astype(jnp.float32)).astype(jnp.bfloat16)

    def masked(tile, keep):
        return (tile.reshape(BLOCK // 16, 16, BLOCK) * mask_tile(keep)[None]).reshape(BLOCK, BLOCK)

    blocks = CHUNK // BLOCK

    def partial_sums(s, way):
        pos = pos_of(way)
        j = s - SKEW_SUM * pos

        @pl.when((j >= 0) & (j < per_way))
        def _():
            slot = lax.rem(j, SLOTS)
            for copy in weight_copies(way, j):
                copy.wait()
            first = (way * per_way + j) * blocks

            @pl.loop(0, depth // BLOCK)
            def _(k):
                top = pl.multiple_of(k * BLOCK, BLOCK)
                for side, keeps in enumerate((gate_keep, up_keep)):
                    for b in range(blocks):
                        lanes = slice((side * blocks + b) * BLOCK, (side * blocks + b + 1) * BLOCK)
                        weights[way, slot, pl.ds(top, BLOCK), lanes] = masked(
                            weights[way, slot, pl.ds(top, BLOCK), lanes], keeps[k, first + b]
                        )

            own[way] = jnp.dot(
                rows[...], weights[way, slot], preferred_element_type=jnp.float32
            )

            @pl.when(j + SLOTS < per_way)
            def _():
                for copy in weight_copies(way, j + SLOTS):
                    copy.start()

    def pass_sums(s, way):
        pos = pos_of(way)
        j = s - SKEW_SUM * pos

        @pl.when((j >= 0) & (j < per_way))
        def _():
            @pl.when(pos == 0)
            def _():
                sums[way, j] = own[way].astype(jnp.bfloat16)

            @pl.when(pos > 0)
            def _():
                sum_copy(way, j).wait_recv()

            @pl.when((pos > 0) & (pos < n - 1))
            def _():
                sums[way, j] = (sums[way, j].astype(jnp.float32) + own[way]).astype(jnp.bfloat16)

            @pl.when(pos < n - 1)
            def _():
                sum_copy(way, j).start()

            @pl.when(pos == n - 1)
            def _():
                gate = sums[way, j, :, :CHUNK].astype(jnp.float32) + own[way, :, :CHUNK]
                up = sums[way, j, :, CHUNK:].astype(jnp.float32) + own[way, :, CHUNK:]
                hid[way, j] = (gate / (1.0 + jnp.exp(-gate)) * up).astype(jnp.bfloat16)

    def hid_index(s, pos):
        return s - SKEW_SUM * (n - 1) - SKEW_HID * (n - 1 - pos)

    def pass_hidden(s, way):
        pos = pos_of(way)
        j = hid_index(s, pos)

        @pl.when((j >= 0) & (j < per_way))
        def _():
            @pl.when(pos < n - 1)
            def _():
                hid_copy(way, j).wait_recv()

            @pl.when(pos > 0)
            def _():
                hid_copy(way, j).start()

    def mix(s, way):
        pos = pos_of(way)
        j = hid_index(s, pos)

        @pl.when((j >= 0) & (j < per_way))
        def _():
            down_copy(way, j).wait()
            first = (way * per_way + j) * blocks
            span = min(256, width)

            @pl.loop(0, width // span)
            def _(c):
                for q in range(span // BLOCK):
                    lanes = pl.ds(pl.multiple_of(c * span + q * BLOCK, BLOCK), BLOCK)
                    for b in range(blocks):
                        down[way, j, b * BLOCK:(b + 1) * BLOCK, lanes] = masked(
                            down[way, j, b * BLOCK:(b + 1) * BLOCK, lanes],
                            down_keep[first + b, c * (span // BLOCK) + q],
                        )
                lanes = pl.ds(pl.multiple_of(c * span, BLOCK), span)
                total[:, lanes] += jnp.dot(
                    hid[way, j], down[way, j, :, lanes], preferred_element_type=jnp.float32
                )

    def fetch_down(s, way):
        @pl.when(s < per_way)
        def _():
            down_copy(way, s).start()

    last = per_way + (SKEW_SUM + SKEW_HID) * (n - 1)

    @pl.loop(0, last)
    def _(s):
        for part in (partial_sums, pass_sums, pass_hidden, fetch_down, mix):
            @pl.loop(0, 2)
            def _(way):
                part(s, way)

    for step in range(1, peers):
        who = lax.rem(y + step, peers)
        leaving[who] = total[pl.ds(pl.multiple_of(who * own_rows, 8), own_rows), :].astype(jnp.bfloat16)
        out_copy(y, who).start()

    for step in range(1, peers):
        row_copy(y, lax.rem(y + step, peers)).wait_send()

    @pl.loop(0, per_way)
    def _(j):
        @pl.loop(0, 2)
        def _(way):
            pos = pos_of(way)

            @pl.when(pos < n - 1)
            def _():
                sum_copy(way, j).wait_send()

            @pl.when(pos > 0)
            def _():
                hid_copy(way, j).wait_send()

    result = total[pl.ds(pl.multiple_of(y * own_rows, 8), own_rows), :]
    for step in range(1, peers):
        who = lax.rem(y + step, peers)
        out_copy(who, y).wait_recv()
        result = result + landing[who].astype(jnp.float32)
    out_ref[...] = result.astype(out_ref.dtype)
    for step in range(1, peers):
        out_copy(y, lax.rem(y + step, peers)).wait_send()


def per_device(n, peers, rows_in, gate_weight, up_weight, down_weight, gate_keep, up_keep, down_keep):
    own_rows, depth = rows_in.shape
    all_rows = own_rows * peers
    hidden, width = down_weight.shape
    per_way = hidden // CHUNK // 2
    bf16, f32 = jnp.bfloat16, jnp.float32
    dma = pltpu.SemaphoreType.DMA
    hbm = pl.BlockSpec(memory_space=pl.ANY)
    smem = pl.BlockSpec(memory_space=pltpu.SMEM)
    return pl.pallas_call(
        functools.partial(ffn_kernel, n, peers, per_way),
        out_shape=jax.ShapeDtypeStruct((own_rows, width), bf16),
        in_specs=[hbm] * 4 + [smem] * 3,
        out_specs=pl.BlockSpec(memory_space=pltpu.VMEM),
        scratch_shapes=[
            pltpu.VMEM((peers, own_rows, depth), bf16),
            pltpu.VMEM((all_rows, depth), bf16),
            pltpu.VMEM((2, SLOTS, depth, 2 * CHUNK), bf16),
            pltpu.VMEM((2, per_way, CHUNK, width), bf16),
            pltpu.VMEM((2, per_way, all_rows, 2 * CHUNK), bf16),
            pltpu.VMEM((2, all_rows, 2 * CHUNK), f32),
            pltpu.VMEM((2, per_way, all_rows, CHUNK), bf16),
            pltpu.VMEM((all_rows, width), f32),
            pltpu.VMEM((peers, own_rows, width), bf16),
            pltpu.VMEM((peers, own_rows, width), bf16),
            dma((peers,)), dma((peers,)), dma,
            dma((2, SLOTS, 2)), dma((2, per_way)),
            dma((2, per_way)), dma((2, per_way)),
            dma((2, per_way)), dma((2, per_way)),
            dma((peers,)), dma((peers,)),
        ],
        compiler_params=pltpu.CompilerParams(
            collective_id=0, has_side_effects=True, vmem_limit_bytes=58 * 1024 * 1024
        ),
    )(rows_in, gate_weight, up_weight, down_weight, gate_keep, up_keep, down_keep)


def solution(mesh):
    in_specs = (
        P(("groups", "gy"), "gx"),
        P("gx", "gy"),
        P("gx", "gy"),
        P("gy", "gx"),
        P("gx", "gy"),
        P("gx", "gy"),
        P("gy", "gx"),
    )
    out_specs = P(("groups", "gy"), "gx")
    body = functools.partial(per_device, mesh.shape["gx"], mesh.shape["gy"])
    return jax.shard_map(body, mesh=mesh, in_specs=in_specs, out_specs=out_specs, check_vma=False)
```

```python
import functools

import jax
import jax.numpy as jnp
from jax import lax
from jax.experimental import pallas as pl
from jax.experimental.pallas import tpu as pltpu
from jax.sharding import PartitionSpec as P

BLOCK = 128
CHUNK = 128
SLOTS = 4
SKEW_SUM = 2
SKEW_HID = 2
MESH = pl.DeviceIdType.MESH


def ffn_kernel(
    n, peers, steps_per_way,
    x_ref, gate_ref, up_ref, down_ref, gate_keep, up_keep, down_keep,
    out_ref,
    gathered, rows, weights, down, sums, own, hid, total, leaving, landing,
    row_send, row_recv, row_local, weight_sem, down_sem,
    sum_send, sum_recv, hid_send, hid_recv, out_send, out_recv,
):
    z = lax.axis_index("gx")
    y = lax.axis_index("gy")
    own_rows, depth = x_ref.shape
    all_rows = peers * own_rows
    width = down_ref.shape[1]
    per_way = steps_per_way

    def pos_of(way):
        return jnp.where(way == 0, z, n - 1 - z)

    def onward(way):
        return jnp.where(way == 0, z + 1, z - 1)

    def backward(way):
        return jnp.where(way == 0, z - 1, z + 1)

    def weight_copies(way, j):
        slot = lax.rem(j, SLOTS)
        start = pl.multiple_of((way * per_way + j) * CHUNK, CHUNK)
        return [
            pltpu.make_async_copy(
                source.at[:, pl.ds(start, CHUNK)],
                weights.at[way, slot, :, pl.ds(side * CHUNK, CHUNK)],
                weight_sem.at[way, slot, side],
            )
            for side, source in enumerate((gate_ref, up_ref))
        ]

    def down_copy(way, j):
        start = pl.multiple_of((way * per_way + j) * CHUNK, CHUNK)
        return pltpu.make_async_copy(
            down_ref.at[pl.ds(start, CHUNK), :], down.at[way, j], down_sem.at[way, j]
        )

    def sum_copy(way, j):
        return pltpu.make_async_remote_copy(
            sums.at[way, j], sums.at[way, j], sum_send.at[way, j], sum_recv.at[way, j],
            device_id={"gx": onward(way)}, device_id_type=MESH,
        )

    def hid_copy(way, j):
        return pltpu.make_async_remote_copy(
            hid.at[way, j], hid.at[way, j], hid_send.at[way, j], hid_recv.at[way, j],
            device_id={"gx": backward(way)}, device_id_type=MESH,
        )

    def row_copy(sender, receiver):
        return pltpu.make_async_remote_copy(
            x_ref, gathered.at[sender], row_send.at[receiver], row_recv.at[sender],
            device_id={"gy": receiver}, device_id_type=MESH,
        )

    def out_copy(sender, receiver):
        return pltpu.make_async_remote_copy(
            leaving.at[receiver], landing.at[sender], out_send.at[receiver], out_recv.at[sender],
            device_id={"gy": receiver}, device_id_type=MESH,
        )

    barrier = pltpu.get_barrier_semaphore()
    for step in range(1, peers):
        pl.semaphore_signal(
            barrier, inc=1, device_id={"gy": lax.rem(y + step, peers)}, device_id_type=MESH
        )

    @pl.when(z > 0)
    def _():
        pl.semaphore_signal(barrier, inc=1, device_id={"gx": z - 1}, device_id_type=MESH)

    @pl.when(z < n - 1)
    def _():
        pl.semaphore_signal(barrier, inc=1, device_id={"gx": z + 1}, device_id_type=MESH)

    local = pltpu.make_async_copy(x_ref, gathered.at[y], row_local)
    local.start()
    for way in range(2):
        for j in range(min(SLOTS, per_way)):
            for copy in weight_copies(way, j):
                copy.start()
    pl.semaphore_wait(barrier, peers - 1 + jnp.where(z > 0, 1, 0) + jnp.where(z < n - 1, 1, 0))

    for step in range(1, peers):
        row_copy(y, lax.rem(y + step, peers)).start()
    local.wait()
    total[...] = jnp.zeros_like(total)
    for step in range(1, peers):
        row_copy(lax.rem(y + step, peers), y).wait_recv()
    if own_rows % 16 == 0:
        for part in range(peers):
            rows[part * own_rows:(part + 1) * own_rows, :] = gathered[part]
    else:
        rows[...] = jnp.concatenate(
            [gathered[part].astype(jnp.float32) for part in range(peers)], axis=0
        ).astype(rows.dtype)

    def mask_tile(keep):
        return jnp.full((16, BLOCK), keep.astype(jnp.float32)).astype(jnp.bfloat16)

    def masked(tile, keep):
        return (tile.reshape(BLOCK // 16, 16, BLOCK) * mask_tile(keep)[None]).reshape(BLOCK, BLOCK)

    blocks = CHUNK // BLOCK

    def partial_sums(s, way):
        pos = pos_of(way)
        j = s - SKEW_SUM * pos

        @pl.when((j >= 0) & (j < per_way))
        def _():
            slot = lax.rem(j, SLOTS)
            for copy in weight_copies(way, j):
                copy.wait()
            first = (way * per_way + j) * blocks

            @pl.loop(0, depth // BLOCK, unroll=min(4, depth // BLOCK))
            def _(k):
                top = pl.multiple_of(k * BLOCK, BLOCK)
                for side, keeps in enumerate((gate_keep, up_keep)):
                    for b in range(blocks):
                        lanes = slice((side * blocks + b) * BLOCK, (side * blocks + b + 1) * BLOCK)
                        weights[way, slot, pl.ds(top, BLOCK), lanes] = masked(
                            weights[way, slot, pl.ds(top, BLOCK), lanes], keeps[k, first + b]
                        )

            own[way] = jnp.dot(
                rows[...], weights[way, slot], preferred_element_type=jnp.float32
            )

            @pl.when(j + SLOTS < per_way)
            def _():
                for copy in weight_copies(way, j + SLOTS):
                    copy.start()

    def pass_sums(s, way):
        pos = pos_of(way)
        j = s - SKEW_SUM * pos

        @pl.when((j >= 0) & (j < per_way))
        def _():
            @pl.when(pos == 0)
            def _():
                sums[way, j] = own[way].astype(jnp.bfloat16)

            @pl.when(pos > 0)
            def _():
                sum_copy(way, j).wait_recv()

            @pl.when((pos > 0) & (pos < n - 1))
            def _():
                sums[way, j] = (sums[way, j].astype(jnp.float32) + own[way]).astype(jnp.bfloat16)

            @pl.when(pos < n - 1)
            def _():
                sum_copy(way, j).start()

            @pl.when(pos == n - 1)
            def _():
                gate = sums[way, j, :, :CHUNK].astype(jnp.float32) + own[way, :, :CHUNK]
                up = sums[way, j, :, CHUNK:].astype(jnp.float32) + own[way, :, CHUNK:]
                hid[way, j] = (gate / (1.0 + jnp.exp(-gate)) * up).astype(jnp.bfloat16)

    def hid_index(s, pos):
        return s - SKEW_SUM * (n - 1) - SKEW_HID * (n - 1 - pos)

    def pass_hidden(s, way):
        pos = pos_of(way)
        j = hid_index(s, pos)

        @pl.when((j >= 0) & (j < per_way))
        def _():
            @pl.when(pos < n - 1)
            def _():
                hid_copy(way, j).wait_recv()

            @pl.when(pos > 0)
            def _():
                hid_copy(way, j).start()

    def mix(s, way):
        pos = pos_of(way)
        j = hid_index(s, pos)

        @pl.when((j >= 0) & (j < per_way))
        def _():
            down_copy(way, j).wait()
            first = (way * per_way + j) * blocks

            @pl.loop(0, width // BLOCK, unroll=min(4, width // BLOCK))
            def _(c):
                lanes = pl.ds(pl.multiple_of(c * BLOCK, BLOCK), BLOCK)
                for b in range(blocks):
                    down[way, j, b * BLOCK:(b + 1) * BLOCK, lanes] = masked(
                        down[way, j, b * BLOCK:(b + 1) * BLOCK, lanes], down_keep[c, first + b]
                    )

            total[...] += jnp.dot(hid[way, j], down[way, j], preferred_element_type=jnp.float32)

    def fetch_down(s, way):
        @pl.when(s < per_way)
        def _():
            down_copy(way, s).start()

    last = per_way + (SKEW_SUM + SKEW_HID) * (n - 1)

    @pl.loop(0, last)
    def _(s):
        for part in (partial_sums, pass_sums, pass_hidden, fetch_down, mix):
            @pl.loop(0, 2)
            def _(way):
                part(s, way)

    for step in range(1, peers):
        who = lax.rem(y + step, peers)
        leaving[who] = total[pl.ds(pl.multiple_of(who * own_rows, 8), own_rows), :].astype(jnp.bfloat16)
        out_copy(y, who).start()

    for step in range(1, peers):
        row_copy(y, lax.rem(y + step, peers)).wait_send()

    @pl.loop(0, per_way)
    def _(j):
        @pl.loop(0, 2)
        def _(way):
            pos = pos_of(way)

            @pl.when(pos < n - 1)
            def _():
                sum_copy(way, j).wait_send()

            @pl.when(pos > 0)
            def _():
                hid_copy(way, j).wait_send()

    result = total[pl.ds(pl.multiple_of(y * own_rows, 8), own_rows), :]
    for step in range(1, peers):
        who = lax.rem(y + step, peers)
        out_copy(who, y).wait_recv()
        result = result + landing[who].astype(jnp.float32)
    out_ref[...] = result.astype(out_ref.dtype)
    for step in range(1, peers):
        out_copy(y, lax.rem(y + step, peers)).wait_send()


def per_device(n, peers, rows_in, gate_weight, up_weight, down_weight, gate_keep, up_keep, down_keep):
    own_rows, depth = rows_in.shape
    all_rows = own_rows * peers
    hidden, width = down_weight.shape
    per_way = hidden // CHUNK // 2
    bf16, f32 = jnp.bfloat16, jnp.float32
    dma = pltpu.SemaphoreType.DMA
    hbm = pl.BlockSpec(memory_space=pl.ANY)
    smem = pl.BlockSpec(memory_space=pltpu.SMEM)
    return pl.pallas_call(
        functools.partial(ffn_kernel, n, peers, per_way),
        out_shape=jax.ShapeDtypeStruct((own_rows, width), bf16),
        in_specs=[hbm] * 4 + [smem] * 3,
        out_specs=pl.BlockSpec(memory_space=pltpu.VMEM),
        scratch_shapes=[
            pltpu.VMEM((peers, own_rows, depth), bf16),
            pltpu.VMEM((all_rows, depth), bf16),
            pltpu.VMEM((2, SLOTS, depth, 2 * CHUNK), bf16),
            pltpu.VMEM((2, per_way, CHUNK, width), bf16),
            pltpu.VMEM((2, per_way, all_rows, 2 * CHUNK), bf16),
            pltpu.VMEM((2, all_rows, 2 * CHUNK), f32),
            pltpu.VMEM((2, per_way, all_rows, CHUNK), bf16),
            pltpu.VMEM((all_rows, width), f32),
            pltpu.VMEM((peers, own_rows, width), bf16),
            pltpu.VMEM((peers, own_rows, width), bf16),
            dma((peers,)), dma((peers,)), dma,
            dma((2, SLOTS, 2)), dma((2, per_way)),
            dma((2, per_way)), dma((2, per_way)),
            dma((2, per_way)), dma((2, per_way)),
            dma((peers,)), dma((peers,)),
        ],
        compiler_params=pltpu.CompilerParams(
            collective_id=0, has_side_effects=True, vmem_limit_bytes=58 * 1024 * 1024
        ),
    )(rows_in, gate_weight, up_weight, down_weight, gate_keep, up_keep, down_keep.T)


def solution(mesh):
    in_specs = (
        P(("groups", "gy"), "gx"),
        P("gx", "gy"),
        P("gx", "gy"),
        P("gy", "gx"),
        P("gx", "gy"),
        P("gx", "gy"),
        P("gy", "gx"),
    )
    out_specs = P(("groups", "gy"), "gx")
    body = functools.partial(per_device, mesh.shape["gx"], mesh.shape["gy"])
    return jax.shard_map(body, mesh=mesh, in_specs=in_specs, out_specs=out_specs, check_vma=False)
```
